32 devices in a mesh: ctx: 8 (over z, y), wa: 4 (over x, core).
Axes of the slice: x: 2, y: 2, z: 4, core: 2. Of those that a mesh axis runs over, the one named last changes fastest.
Arguments:
- tokens: bfloat16 [8, 1024, 960], P('wa', 'ctx'), may hold values from -6 to 6
- w_query: bfloat16 [960, 960], P('wa'), may hold values from -0.1875 to 0.1875
- w_key: bfloat16 [960, 320], P('wa'), may hold values from -0.1875 to 0.1875
- w_value: bfloat16 [960, 320], P('wa'), may hold values from -0.1875 to 0.1875
- w_out: bfloat16 [960, 960], P('wa'), may hold values from -1.5 to 1.5
- w_gate: bfloat16 [960, 2560], P('wa'), may hold values from -0.1875 to 0.1875
- w_up: bfloat16 [960, 2560], P('wa'), may hold values from -0.1875 to 0.1875
- w_down: bfloat16 [2560, 960], P('wa'), may hold values from -0.125 to 0.125
- norm_attn: bfloat16 [960], P('wa'), may hold values from 0.5 to 1.5
- norm_ffn: bfloat16 [960], P('wa'), may hold values from 0.5 to 1.5
- cotangent: bfloat16 [8, 1024, 960], P('wa', 'ctx'), may hold values from -6 to 6
Outputs:
- mixed: bfloat16 [8, 1024, 960], P('wa', 'ctx')
- input_grad: bfloat16 [8, 1024, 960], P('wa', 'ctx')
- grad_query: float32 [960, 960], P('wa')
- grad_key: float32 [960, 320], P('wa')
- grad_value: float32 [960, 320], P('wa')
- grad_out: float32 [960, 960], P('wa')
- grad_gate: float32 [960, 2560], P('wa')
- grad_up: float32 [960, 2560], P('wa')
- grad_down: float32 [2560, 960], P('wa')
- grad_norm_attn: float32 [960], P('wa')
- grad_norm_ffn: float32 [960], P('wa')
The draws below stay inside these ranges and needn't reach their ends.
All inputs are finite; a program needn't handle non-finite values.
Results may differ from the reference program's by a relative error of at most 0.018.
Values may be sent and summed in bfloat16 or wider, within the bound.
No kernel may reach another device: no remote copies, remote signals or barrier semaphores. Data moves between devices by JAX's collectives and lax.ppermute only.
A program may use at most 192 MiB of HBM per device.

```python
import jax
import jax.numpy as jnp
from jax import lax

D = 960
HEADS = 15
KV_HEADS = 5
HEAD = 64
FF = 2560
KEYB = 512
SEQS = 8
LEN = 1024


def levels(rng, shape, pieces, low, largest):
    loudness, own = 1.0, jax.random.fold_in(rng, 6)
    for dim, blocks in pieces:
        draws = jnp.exp(jax.random.uniform(jax.random.fold_in(own, dim), (blocks,), jnp.float32, low / len(pieces), largest / len(pieces)))
        loudness = loudness * jnp.repeat(draws, shape[dim] // blocks).reshape([-1 if axis == dim else 1 for axis in range(len(shape))])
    return loudness


def bell_draw(own_key, extent, width, reach, split=(), dtype=jnp.bfloat16):
    array = jax.random.normal(own_key, extent, jnp.float32) * width
    if len(split) > 0:
        array = levels(own_key, extent, split, -0.22, 0.18) * array
    return jnp.clip(array, min=-reach, max=reach).astype(dtype)


def setup_inputs(seed: int = 0) -> dict:
    seeds = jax.random.split(jax.random.key(seed), 12)
    return {
        "tokens": bell_draw(seeds[0], (SEQS, LEN, D), 1.0, 6.0, ((0, 4), (1, 8))),
        "w_query": bell_draw(seeds[1], (D, HEADS * HEAD), D ** -0.5, 0.1875, ((0, 4),)),
        "w_key": bell_draw(seeds[2], (D, KV_HEADS * HEAD), D ** -0.5, 0.1875, ((0, 4),)),
        "w_value": bell_draw(seeds[3], (D, KV_HEADS * HEAD), D ** -0.5, 0.1875, ((0, 4),)),
        "w_out": bell_draw(seeds[4], (HEADS * HEAD, D), 16 ** -0.5, 1.5, ((0, 4),)),
        "w_gate": bell_draw(seeds[5], (D, FF), D ** -0.5, 0.1875, ((0, 4),)),
        "w_up": bell_draw(seeds[6], (D, FF), D ** -0.5, 0.1875, ((0, 4),)),
        "w_down": bell_draw(seeds[7], (FF, D), FF ** -0.5, 0.125, ((0, 4),)),
        "norm_attn": jnp.clip(1.0 + 0.1 * jax.random.normal(seeds[8], (D,), jnp.float32), 0.5, 1.5).astype(jnp.bfloat16),
        "norm_ffn": jnp.clip(1.0 + 0.1 * jax.random.normal(seeds[9], (D,), jnp.float32), 0.5, 1.5).astype(jnp.bfloat16),
        "cotangent": bell_draw(seeds[10], (SEQS, LEN, D), 1.0, 6.0, ((0, 4), (1, 8))),
    }


@jax.custom_vjp
def low(v):
    return lax.optimization_barrier(v.astype(jnp.bfloat16)).astype(jnp.float32)

@jax.custom_vjp
def low_back(v):
    return v

def low_keep(v):
    return (low(v), None)

def low_pass(kept, grad):
    return (grad,)

def back_keep(v):
    return (v, None)

def back_low(kept, grad):
    return (low(grad),)
low.defvjp(low_keep, low_pass)
low_back.defvjp(back_keep, back_low)
epsilon = 1e-05
highest = lax.Precision.HIGHEST

def rms_scale(values_in, gain_vec):
    return values_in * lax.rsqrt(lax.optimization_barrier(jnp.mean(values_in * values_in, axis=-1, keepdims=True)) + epsilon) * gain_vec

def rotate(values_in, position):
    half_size = values_in.shape[-1] // 2
    frequency = 10000.0 ** (-jnp.arange(half_size).astype(jnp.float32) / half_size)
    angles = position[:, None] * frequency[None, :]
    cosines = jnp.cos(angles)[:, None, :]
    sines = jnp.sin(angles)[:, None, :]
    front_half = values_in[..., :half_size]
    back_half = values_in[..., half_size:]
    return jnp.concatenate([front_half * cosines - back_half * sines, back_half * cosines + front_half * sines], axis=-1)

def layer(source, w_query, w_key, w_value, w_out, w_gate, w_up, w_down, gain_attn, gain_ffn):
    length = source.shape[0]
    per_group = HEADS // KV_HEADS
    position = jnp.arange(length).astype(jnp.float32)
    normed = low(rms_scale(source, gain_attn))
    query_raw = low_back(jnp.dot(normed, w_query, precision=highest)).reshape(length, HEADS, HEAD)
    queries = low(rotate(query_raw, position)).reshape(length, KV_HEADS, per_group, HEAD)
    key_raw = low_back(jnp.dot(normed, w_key, precision=highest)).reshape(length, KV_HEADS, HEAD)
    keys = low(rotate(key_raw, position))
    values = low(low_back(jnp.dot(normed, w_value, precision=highest))).reshape(length, KV_HEADS, HEAD)
    blocks = length // KEYB
    query_blocks = queries.reshape(blocks, KEYB, KV_HEADS, per_group, HEAD)
    block_starts = (jnp.arange(blocks) * KEYB).astype(jnp.int32)
    key_places = jnp.arange(length).astype(jnp.int32)

    def attend(block_item):
        query_block, block_start = block_item
        score = low_back(jnp.einsum('tgrd,kgd->tgrk', query_block, keys, precision=highest) * HEAD ** (-0.5))
        row_places = block_start + jnp.arange(KEYB).astype(jnp.int32)
        allowed = (key_places[None, :] <= row_places[:, None])[:, None, None, :]
        score = jnp.where(allowed, score, -1e+30)
        row_max = lax.optimization_barrier(jnp.max(score, axis=-1, keepdims=True))
        log_total = row_max + jnp.log(lax.optimization_barrier(jnp.sum(jnp.exp(score - row_max), axis=-1, keepdims=True)))
        softmax_p = low(jnp.exp(score - log_total))
        return jnp.einsum('tgrk,kgd->tgrd', softmax_p, values, precision=highest)
    attended = lax.map(jax.checkpoint(attend), (query_blocks, block_starts))
    heads_out = low(low_back(attended.reshape(length, HEADS * HEAD)))
    resid_mid = source + low_back(jnp.dot(heads_out, w_out, precision=highest))
    normed_two = low(rms_scale(resid_mid, gain_ffn))
    gate = low_back(jnp.dot(normed_two, w_gate, precision=highest))
    up_part = low_back(jnp.dot(normed_two, w_up, precision=highest))
    activated = low(jax.nn.silu(gate) * up_part)
    return resid_mid + low_back(jnp.dot(activated, w_down, precision=highest))

def reference(tokens, w_query, w_key, w_value, w_out, w_gate, w_up, w_down, norm_attn, norm_ffn, cotangent):
    weights = tuple((w_item.astype(jnp.float32) for w_item in (w_query, w_key, w_value, w_out, w_gate, w_up, w_down, norm_attn, norm_ffn)))

    def one_sequence(totals, sequence_item):
        sequence, grad_output = sequence_item
        result, pullback = jax.vjp(layer, sequence.astype(jnp.float32), *weights)
        gradients = pullback(grad_output.astype(jnp.float32))
        totals = tuple((left + right for left, right in zip(totals, gradients[1:])))
        return (totals, (result.astype(jnp.bfloat16), gradients[0].astype(jnp.bfloat16)))
    initial = tuple((jnp.zeros(w_item.shape, jnp.float32) for w_item in weights))
    totals, outputs = lax.scan(one_sequence, initial, (tokens, cotangent))
    return (outputs[0], outputs[1], totals[0], totals[1], totals[2], totals[3], totals[4], totals[5], totals[6], totals[7], totals[8])
```

```python
import functools

import jax
import jax.numpy as jnp
from jax import lax
from jax.experimental import pallas as pl
from jax.experimental.pallas import tpu as pltpu
from jax.sharding import PartitionSpec as P

HEAD = 64
EPS = 1e-05
BF = jnp.bfloat16
F32 = jnp.float32
VMEM_LIMIT = 60 * 1024 * 1024


def mm(a, b, ca, cb):
    return lax.dot_general(a, b, (((ca,), (cb,)), ((), ())), preferred_element_type=F32)


def bits_of(n):
    return max(n - 1, 0).bit_length()


def swap(a, axis, n, bit):
    return lax.ppermute(a, axis, [(i, i ^ (1 << bit)) for i in range(n)])


def my_bit(axis, bit):
    return (lax.axis_index(axis) >> bit) & 1


def ordered(mine, theirs, bit, dim):
    return jnp.where(
        bit == 0,
        jnp.concatenate([mine, theirs], axis=dim),
        jnp.concatenate([theirs, mine], axis=dim),
    )


def gather_rows(a, n):
    nb = bits_of(n)
    out = a.reshape((1,) * nb + a.shape)
    for bit in reversed(range(nb)):
        dim = nb - 1 - bit
        out = ordered(out, swap(out, "wa", n, bit), my_bit("wa", bit), dim)
    return out.reshape((n,) + a.shape)


def gather_relative(a, n):
    blocks = {0: a}
    for bit in reversed(range(bits_of(n))):
        for place in list(blocks):
            blocks[place | (1 << bit)] = swap(blocks[place], "wa", n, bit)
    return jnp.concatenate(list(blocks.values()), axis=0)


def scatter_relative(a, n):
    for bit in range(bits_of(n)):
        half = a.shape[0] // 2
        a = a[:half] + swap(a[half:].astype(BF), "wa", n, bit).astype(F32)
    return a


def scatter_rows(a, n):
    nb = bits_of(n)
    a = a.reshape((2,) * nb + a.shape[1:])
    for bit in range(nb):
        dim = nb - 1 - bit
        mine = my_bit("wa", bit)
        keep = lax.dynamic_slice_in_dim(a, mine, 1, dim)
        send = lax.dynamic_slice_in_dim(a, 1 - mine, 1, dim).astype(BF)
        a = (keep.astype(F32) + swap(send, "wa", n, bit).astype(F32)).astype(BF)
    return a.reshape(a.shape[nb:])


def exchange_blocks(take, n, place):
    me = lax.axis_index("wa")
    result = place(None, take(me), me)
    for step in range(1, n):
        got = lax.ppermute(take(me ^ step), "wa", [(i, i ^ step) for i in range(n)])
        result = place(result, got, me ^ step)
    return result


def reduce_halves(a, n, plan):
    trail = []
    for bit, dim in plan:
        size = a.shape[dim]
        half = -(-size // 16) * 8
        mine = my_bit("ctx", bit)
        if half >= size:
            got = swap(a.astype(BF), "ctx", n, bit)
            a = (a.astype(F32) + got.astype(F32)).astype(BF)
            trail.append((bit, dim, None))
            continue
        keep = lax.dynamic_slice_in_dim(a, mine * (size - half), half, dim)
        send = lax.dynamic_slice_in_dim(a, (1 - mine) * (size - half), half, dim).astype(BF)
        a = (keep.astype(F32) + swap(send, "ctx", n, bit).astype(F32)).astype(BF)
        trail.append((bit, dim, size))
    return a, trail


def gather_halves(a, n, trail):
    for bit, dim, size in reversed(trail):
        if size is None:
            continue
        got = swap(a, "ctx", n, bit)
        mine = my_bit("ctx", bit)
        if 2 * a.shape[dim] == size:
            a = ordered(a, got, mine, dim)
        else:
            low = jnp.where(mine == 0, a, got)
            high = jnp.where(mine == 0, got, a)
            extra = 2 * a.shape[dim] - size
            high = lax.slice_in_dim(high, extra, a.shape[dim], axis=dim)
            a = jnp.concatenate([low, high], axis=dim)
    return a


def all_reduce_ctx(a, n, plan):
    part, trail = reduce_halves(a, n, plan)
    return gather_halves(part, n, trail)


def doubled(a, n, order):
    for bit in order:
        a = jnp.concatenate([a, swap(a, "ctx", n, bit)], axis=0)
    return a


def halved(a, n, order):
    for bit in reversed(order):
        half = a.shape[0] // 2
        got = swap(a[half:], "ctx", n, bit)
        a = (a[:half].astype(F32) + got.astype(F32)).astype(BF if half > 1 else F32)
    return a


def slot_offsets(order):
    offsets = [0]
    for bit in order:
        offsets = offsets + [offset ^ (1 << bit) for offset in offsets]
    return offsets


def group_columns(ref, group, per_group):
    return jnp.concatenate(
        [
            ref[(group * per_group + r) * HEAD : (group * per_group + r + 1) * HEAD, :]
            for r in range(per_group)
        ],
        axis=1,
    )


def slot_columns(ref, first, count, row):
    return jnp.concatenate(
        [ref[first + s, row : row + HEAD, :] for s in range(count)], axis=1
    )


def attend_kernel(groups, per_group, chunk, q_ref, kv_ref, bias_ref, o_ref, lse_ref):
    rows = q_ref.shape[1]
    slots = kv_ref.shape[0]
    wide = per_group * rows
    for group in range(groups):
        q = group_columns(q_ref, group, per_group)

        def step(index, running):
            first = index * chunk
            k = slot_columns(kv_ref, first, chunk, group * HEAD)
            v = slot_columns(kv_ref, first, chunk, (groups + group) * HEAD)
            bias = bias_ref[pl.ds(first * rows, chunk * rows), :]
            s = mm(k, q, 0, 0) + jnp.concatenate([bias] * per_group, axis=1)
            top = jnp.max(s, axis=0, keepdims=True)
            if running is not None:
                top = jnp.maximum(top, running[0])
            p = jnp.exp(s - top)
            total = jnp.sum(p, axis=0, keepdims=True)
            out = mm(v, p.astype(BF), 1, 0)
            if running is not None:
                shrink = jnp.exp(running[0] - top)
                total = total + running[1] * shrink
                out = out + running[2] * shrink
            return (top, total, out)

        if slots == chunk:
            top, total, out = step(0, None)
        else:
            top, total, out = lax.fori_loop(
                0,
                slots // chunk,
                step,
                (
                    jnp.full((1, wide), -1e30, F32),
                    jnp.zeros((1, wide), F32),
                    jnp.zeros((HEAD, wide), F32),
                ),
            )
        out = out / total
        lse = top + jnp.log(total)
        for r in range(per_group):
            head = group * per_group + r
            o_ref[head * HEAD : (head + 1) * HEAD, :] = out[:, r * rows : (r + 1) * rows]
            lse_ref[head : head + 1, :] = lse[:, r * rows : (r + 1) * rows]


def attend_back_kernel(
    groups, per_group, chunk, q_ref, kv_ref, bias_ref, lse_ref, do_ref, o_ref, dq_ref, dkv_ref
):
    rows = q_ref.shape[1]
    slots = kv_ref.shape[0]
    wide = per_group * rows
    for group in range(groups):
        q = group_columns(q_ref, group, per_group)
        do = group_columns(do_ref, group, per_group)
        o = group_columns(o_ref, group, per_group)
        delta = jnp.sum(do.astype(F32) * o, axis=0, keepdims=True)
        lse = jnp.concatenate(
            [
                lse_ref[group * per_group + r : group * per_group + r + 1, :]
                for r in range(per_group)
            ],
            axis=1,
        )

        def step(index, dq):
            first = index * chunk
            k = slot_columns(kv_ref, first, chunk, group * HEAD)
            v = slot_columns(kv_ref, first, chunk, (groups + group) * HEAD)
            bias = bias_ref[pl.ds(first * rows, chunk * rows), :]
            s = mm(k, q, 0, 0) + jnp.concatenate([bias] * per_group, axis=1)
            p = jnp.exp(s - lse)
            dp = mm(v, do, 0, 0)
            ds = (p * (dp - delta)).astype(BF)
            dk = mm(q, ds, 1, 1).astype(BF)
            dv = mm(do, p.astype(BF), 1, 1).astype(BF)
            for s_index in range(chunk):
                columns = slice(s_index * rows, (s_index + 1) * rows)
                dkv_ref[first + s_index, group * HEAD : (group + 1) * HEAD, :] = dk[:, columns]
                dkv_ref[
                    first + s_index, (groups + group) * HEAD : (groups + group + 1) * HEAD, :
                ] = dv[:, columns]
            return dq + mm(k, ds, 1, 0)

        dq = jnp.zeros((HEAD, wide), F32)
        dq = step(0, dq) if slots == chunk else lax.fori_loop(0, slots // chunk, step, dq)
        dq = dq * HEAD ** (-0.5)
        for r in range(per_group):
            head = group * per_group + r
            dq_ref[head * HEAD : (head + 1) * HEAD, :] = dq[:, r * rows : (r + 1) * rows]


def attend(groups, per_group, q, kv, bias):
    rows, slots = q.shape[1], kv.shape[0]
    heads = groups * per_group
    cost = pl.CostEstimate(
        flops=4 * heads * HEAD * rows * rows * slots * 2,
        bytes_accessed=q.size * 6 + kv.size * 2 + bias.size * 4,
        transcendentals=heads * rows * rows * slots,
    )
    return pl.pallas_call(
        functools.partial(attend_kernel, groups, per_group, min(slots, 8)),
        out_shape=(
            jax.ShapeDtypeStruct(q.shape, F32),
            jax.ShapeDtypeStruct((heads, rows), F32),
        ),
        cost_estimate=cost,
        compiler_params=pltpu.CompilerParams(vmem_limit_bytes=VMEM_LIMIT),
    )(q, kv, bias)


def attend_back(groups, per_group, q, kv, bias, lse, do, o):
    rows, slots = q.shape[1], kv.shape[0]
    heads = groups * per_group
    cost = pl.CostEstimate(
        flops=10 * heads * HEAD * rows * rows * slots * 2,
        bytes_accessed=q.size * 12 + kv.size * 4 + bias.size * 4,
        transcendentals=heads * rows * rows * slots,
    )
    return pl.pallas_call(
        functools.partial(attend_back_kernel, groups, per_group, min(slots, 8)),
        out_shape=(
            jax.ShapeDtypeStruct(q.shape, F32),
            jax.ShapeDtypeStruct(kv.shape, BF),
        ),
        cost_estimate=cost,
        compiler_params=pltpu.CompilerParams(vmem_limit_bytes=VMEM_LIMIT),
    )(q, kv, bias, lse, do, o)


def rms(x, gain):
    r = lax.rsqrt(jnp.mean(x * x, axis=-1, keepdims=True) + EPS)
    return x * r * gain, r


def rms_back(dh, x, r, gain):
    xn = x * r
    d_gain = jnp.sum(dh * xn, axis=0)
    dxn = dh * gain
    return r * (dxn - xn * jnp.mean(dxn * xn, axis=-1, keepdims=True)), d_gain


def turn(z, cosines, sines, back=False):
    if back:
        sines = -sines
    half = HEAD // 2
    parts = z.reshape(z.shape[0] // HEAD, HEAD, z.shape[1])
    a, b = parts[:, :half], parts[:, half:]
    return jnp.concatenate([a * cosines - b * sines, b * cosines + a * sines], axis=1).reshape(
        z.shape
    )


def local(
    n_ctx,
    n_wa,
    tokens,
    w_query,
    w_key,
    w_value,
    w_out,
    w_gate,
    w_up,
    w_down,
    norm_attn,
    norm_ffn,
    cotangent,
):
    seqs, rows, width = tokens.shape
    q_width, k_width = w_query.shape[1], w_key.shape[1]
    per_group = q_width // k_width
    groups = k_width // HEAD
    shard = w_query.shape[0]
    ff_part = w_down.shape[0]
    c_bits = bits_of(n_ctx)
    each = range(seqs)
    here = lax.axis_index("ctx")

    gains = gather_rows(jnp.stack([norm_attn, norm_ffn]), n_wa)
    gains = gains.transpose(1, 0, 2).reshape(2, width).astype(F32)
    w_qkv = gather_rows(jnp.concatenate([w_query, w_key, w_value], axis=1), n_wa)
    w_qkv = w_qkv.reshape(width, q_width + 2 * k_width)
    w_o = gather_rows(w_out, n_wa).reshape(q_width, width)

    def take_columns(device):
        return jnp.concatenate(
            [
                lax.dynamic_slice_in_dim(w, device * ff_part, ff_part, 1)
                for w in (w_gate, w_up)
            ],
            axis=1,
        )

    def place_rows(result, block, device):
        if result is None:
            result = jnp.zeros((width, 2 * ff_part), BF)
        return lax.dynamic_update_slice_in_dim(result, block, device * shard, 0)

    w_gu = exchange_blocks(take_columns, n_wa, place_rows)
    dy_all = [gather_relative(cotangent[i], n_wa) for i in each]

    half = HEAD // 2
    frequency = 10000.0 ** (-jnp.arange(half).astype(F32) / half)
    position = (here * rows + jnp.arange(rows, dtype=jnp.int32)).astype(F32)
    angles = frequency[:, None] * position[None, :]
    cosines, sines = lax.optimization_barrier((jnp.cos(angles), jnp.sin(angles)))
    high_first = list(reversed(range(c_bits)))
    low_swapped = high_first[:-2] + high_first[-2:][::-1]
    orders = [high_first if i % 2 == 0 else low_swapped for i in each]

    def bias_of(order):
        block = here ^ jnp.array(slot_offsets(order), jnp.int32)
        key_place = (block[:, None] * rows + jnp.arange(rows, dtype=jnp.int32)[None, :]).reshape(-1)
        query_place = here * rows + jnp.arange(rows, dtype=jnp.int32)
        return jnp.where(key_place[:, None] <= query_place[None, :], 0.0, -1e30).astype(F32)

    biases = [bias_of(order) for order in orders]

    x, h1, r1, q, kv = [], [], [], [], []
    for i in each:
        xi = tokens[i].astype(F32)
        hi, ri = rms(xi, gains[0])
        hi = hi.astype(BF)
        qkv = mm(w_qkv, hi, 0, 1)
        qi = turn(qkv[:q_width], cosines, sines).astype(BF) * BF(HEAD ** (-0.5))
        ki = turn(qkv[q_width : q_width + k_width], cosines, sines).astype(BF)
        vi = qkv[q_width + k_width :].astype(BF)
        x.append(xi)
        h1.append(hi)
        r1.append(ri)
        q.append(qi)
        kv.append(doubled(jnp.concatenate([ki, vi], axis=0)[None], n_ctx, orders[i]))

    o, lse, o_b, x1, r2, h2_all = [], [], [], [], [], []
    for i in each:
        oi, li = attend(groups, per_group, q[i], kv[i], biases[i])
        ob = oi.astype(BF)
        x1i = x[i] + mm(ob, w_o, 0, 0)
        h2, r2i = rms(x1i, gains[1])
        o.append(oi)
        lse.append(li)
        o_b.append(ob)
        x1.append(x1i)
        r2.append(r2i)
        h2_all.append(gather_relative(h2.astype(BF), n_wa))

    mixed, dh2, act_all, dgu_all = [], [], [], []
    for i in each:
        gu = mm(h2_all[i], w_gu, 1, 0)
        gate, up = gu[:, :ff_part], gu[:, ff_part:]
        sig = jax.nn.sigmoid(gate)
        silu = gate * sig
        act = (silu * up).astype(BF)
        dact = mm(dy_all[i], w_down, 1, 1)
        dgate = (dact * up * sig * (1.0 + gate * (1.0 - sig))).astype(BF)
        dup = (dact * silu).astype(BF)
        dgu = jnp.concatenate([dgate, dup], axis=1)
        dh2.append(scatter_relative(mm(dgu, w_gu, 1, 1), n_wa))
        mixed.append((x1[i] + scatter_relative(mm(act, w_down, 1, 0), n_wa)).astype(BF))
        act_all.append(act)
        dgu_all.append(dgu)
    act_all = jnp.concatenate(act_all, axis=0)
    dgu_all = jnp.concatenate(dgu_all, axis=0)
    h2_cat = jnp.concatenate(h2_all, axis=0)
    dy_cat = jnp.concatenate(dy_all, axis=0)

    low_first = list(range(c_bits))
    middle_first = low_first[1:] + low_first[:1]
    g_gu = mm(h2_cat, dgu_all, 0, 0).astype(BF).reshape(n_wa, shard, 2 * ff_part)
    g_down = mm(act_all, dy_cat, 0, 0).astype(BF)
    gu_part, gu_trail = reduce_halves(
        g_gu, n_ctx, [(bit, 2 if index == 0 else 1) for index, bit in enumerate(low_first)]
    )

    def place_sources(result, block, device):
        if result is None:
            result = jnp.zeros_like(gu_part)
        return lax.dynamic_update_slice_in_dim(result, block, device, 0)

    gu_part = exchange_blocks(
        lambda device: lax.dynamic_slice_in_dim(gu_part, device, 1, 0), n_wa, place_sources
    )
    g_gu = gather_halves(gu_part, n_ctx, gu_trail)
    g_gate, g_up = [
        g_gu[:, :, s * ff_part : (s + 1) * ff_part]
        .transpose(1, 0, 2)
        .reshape(shard, n_wa * ff_part)
        .astype(F32)
        for s in range(2)
    ]
    g_down = all_reduce_ctx(g_down, n_ctx, [(bit, 0) for bit in middle_first]).astype(F32)

    dx1, dx1_b, dq_b, dkv, dg2 = [], [], [], [], []
    for i in each:
        norm_part, dgi = rms_back(dh2[i], x1[i], r2[i], gains[1])
        dx1i = cotangent[i].astype(F32) + norm_part
        dx1b = dx1i.astype(BF)
        do = mm(w_o, dx1b, 1, 1).astype(BF)
        dqi, dkvi = attend_back(groups, per_group, q[i], kv[i], biases[i], lse[i], do, o[i])
        dx1.append(dx1i)
        dx1_b.append(dx1b)
        dg2.append(dgi)
        dq_b.append(turn(dqi, cosines, sines, back=True).astype(BF))
        dkv.append(halved(dkvi, n_ctx, orders[i])[0])

    h1_cat = jnp.concatenate(h1, axis=0)
    g_out = mm(jnp.concatenate(o_b, axis=1), jnp.concatenate(dx1_b, axis=0), 1, 0)
    g_query = mm(h1_cat, jnp.concatenate(dq_b, axis=1), 0, 1)
    g_oq = jnp.concatenate([g_out, g_query], axis=1).astype(BF).reshape(n_wa, shard, -1)
    plan = [(bit, 0) for bit in low_first]
    g_oq = all_reduce_ctx(scatter_rows(g_oq, n_wa), n_ctx, plan).astype(F32)

    input_grad, dkv_b, dg1 = [], [], []
    for i in each:
        dk = turn(dkv[i][:k_width], cosines, sines, back=True)
        dkvb = jnp.concatenate([dk, dkv[i][k_width:]], axis=0).astype(BF)
        dh1 = mm(dq_b[i], w_qkv[:, :q_width], 0, 1) + mm(dkvb, w_qkv[:, q_width:], 0, 1)
        norm_part, dgi = rms_back(dh1, x[i], r1[i], gains[0])
        input_grad.append((dx1[i] + norm_part).astype(BF))
        dkv_b.append(dkvb)
        dg1.append(dgi)
    g_kv = mm(h1_cat, jnp.concatenate(dkv_b, axis=1), 0, 1).reshape(n_wa, shard, -1)
    g_gain = jnp.stack([sum(dg1), sum(dg2)]).reshape(2, n_wa, shard).transpose(1, 0, 2)
    g_gain = jnp.pad(g_gain, ((0, 0), (0, 6), (0, g_kv.shape[2] - shard)))
    g_kv = jnp.concatenate([g_kv, g_gain], axis=1).astype(BF)
    g_kv = all_reduce_ctx(scatter_rows(g_kv, n_wa), n_ctx, plan).astype(F32)

    return (
        jnp.stack(mixed),
        jnp.stack(input_grad),
        g_oq[:, width:],
        g_kv[:shard, :k_width],
        g_kv[:shard, k_width:],
        g_oq[:, :width],
        g_gate,
        g_up,
        g_down,
        g_kv[shard, :shard],
        g_kv[shard + 1, :shard],
    )


def solution(mesh):
    rows, weight, vector = P("wa", "ctx", None), P("wa", None), P("wa")
    specs = (weight,) * 7 + (vector,) * 2
    return jax.shard_map(
        functools.partial(local, mesh.shape["ctx"], mesh.shape["wa"]),
        mesh=mesh,
        in_specs=(rows,) + specs + (rows,),
        out_specs=(rows, rows) + specs,
        check_vma=False,
    )
```

```python
import functools

import jax
import jax.numpy as jnp
from jax import lax
from jax.experimental import pallas as pl
from jax.experimental.pallas import tpu as pltpu
from jax.sharding import PartitionSpec as P

HEAD = 64
EPS = 1e-05
BF = jnp.bfloat16
F32 = jnp.float32
VMEM_LIMIT = 60 * 1024 * 1024


def mm(a, b, ca, cb):
    return lax.dot_general(a, b, (((ca,), (cb,)), ((), ())), preferred_element_type=F32)


def bits_of(n):
    return max(n - 1, 0).bit_length()


def swap(a, axis, n, bit):
    return lax.ppermute(a, axis, [(i, i ^ (1 << bit)) for i in range(n)])


def my_bit(axis, bit):
    return (lax.axis_index(axis) >> bit) & 1


def ordered(mine, theirs, bit, dim):
    return jnp.where(
        bit == 0,
        jnp.concatenate([mine, theirs], axis=dim),
        jnp.concatenate([theirs, mine], axis=dim),
    )


def after(value, other):
    return lax.optimization_barrier((value, other))[0]


class Chain:
    def __init__(self, steps):
        self.steps = steps
        self.pending = next(steps)
        self.result = None

    def issue(self, value=None):
        if self.pending is None:
            return value
        if value is not None:
            value = after(value, self.pending)
        try:
            self.pending = self.steps.send(self.pending)
        except StopIteration as stop:
            self.pending, self.result = None, stop.value
        return value

    def finish(self):
        while self.pending is not None:
            self.issue()
        return self.result


def gather_rows(a, n, lead=None):
    lead = lead or a.shape[0]
    nb = bits_of(n)
    out = a.reshape((1,) * nb + a.shape)
    for bit in reversed(range(nb)):
        dim, mine = nb - 1 - bit, my_bit("wa", bit)
        got = swap(out, "wa", n, bit)
        wait = yield got
        got = got if wait is None else after(got, wait)
        if bit == 0:
            rest = ordered(out[..., lead:, :], got[..., lead:, :], mine, dim)
            out, got = out[..., :lead, :], got[..., :lead, :]
        out = ordered(out, got, mine, dim)
    return out.reshape(-1, a.shape[1]), rest.reshape(n, -1, a.shape[1])


def gather_relative(a, n):
    blocks = {0: a}
    for bit in reversed(range(bits_of(n))):
        for place in list(blocks):
            blocks[place | (1 << bit)] = swap(blocks[place], "wa", n, bit)
    return jnp.concatenate(list(blocks.values()), axis=0)


def scatter_relative(a, n):
    for bit in range(bits_of(n)):
        half = a.shape[0] // 2
        a = a[:half] + swap(a[half:].astype(BF), "wa", n, bit).astype(F32)
    return a


def scatter_rows(a, n):
    nb = bits_of(n)
    a = a.reshape((2,) * nb + a.shape[1:])
    for bit in range(nb):
        dim = nb - 1 - bit
        mine = my_bit("wa", bit)
        keep = lax.dynamic_slice_in_dim(a, mine, 1, dim)
        send = lax.dynamic_slice_in_dim(a, 1 - mine, 1, dim).astype(BF)
        send = yield send
        a = (keep.astype(F32) + swap(send, "wa", n, bit).astype(F32)).astype(BF)
    return a.reshape(a.shape[nb:])


def exchange_blocks(a, n):
    nb = bits_of(n)
    out = a.reshape((2,) * nb + a.shape[1:])
    for bit in reversed(range(nb)):
        dim, mine = nb - 1 - bit, my_bit("wa", bit)
        keep = lax.dynamic_slice_in_dim(out, mine, 1, dim)
        got = swap(lax.dynamic_slice_in_dim(out, 1 - mine, 1, dim), "wa", n, bit)
        wait = yield got
        got = got if wait is None else after(got, wait)
        out = ordered(keep, got, mine, dim)
    return out.reshape(a.shape)


def complete(steps, wait=None):
    try:
        steps.send(wait)
        while True:
            next(steps)
    except StopIteration as stop:
        return stop.value


def all_reduce_ctx(a, n, plan):
    trail = []
    for bit in plan:
        size = a.shape[0]
        half = -(-size // 16) * 8
        mine = my_bit("ctx", bit)
        if half >= size:
            send = a.astype(BF)
            yield send
            a = (a.astype(F32) + swap(send, "ctx", n, bit).astype(F32)).astype(BF)
            continue
        keep = lax.dynamic_slice_in_dim(a, mine * (size - half), half, 0)
        send = lax.dynamic_slice_in_dim(a, (1 - mine) * (size - half), half, 0).astype(BF)
        yield send
        a = (keep.astype(F32) + swap(send, "ctx", n, bit).astype(F32)).astype(BF)
        trail.append((bit, size))
    for bit, size in reversed(trail):
        yield a
        got = swap(a, "ctx", n, bit)
        mine = my_bit("ctx", bit)
        extra = 2 * a.shape[0] - size
        if extra == 0:
            a = ordered(a, got, mine, 0)
        else:
            low = jnp.where(mine == 0, a, got)
            high = jnp.where(mine == 0, got, a)
            a = jnp.concatenate([low, high[extra:]], axis=0)
    return a


def all_reduce_rows(a, n_wa, n_ctx, plan):
    own = yield from scatter_rows(a, n_wa)
    return (yield from all_reduce_ctx(own, n_ctx, plan))


def doubled(a, n, order):
    for bit in order:
        yield a
        a = jnp.concatenate([a, swap(a, "ctx", n, bit)], axis=0)
    return a


def halved(a, n, order):
    for bit in reversed(order):
        half = a.shape[0] // 2
        send = yield a[half:]
        got = swap(send, "ctx", n, bit)
        a = (a[:half].astype(F32) + got.astype(F32)).astype(BF if half > 1 else F32)
    return a


def slot_offsets(order):
    offsets = [0]
    for bit in order:
        offsets = offsets + [offset ^ (1 << bit) for offset in offsets]
    return offsets


def group_columns(ref, group, per_group):
    return jnp.concatenate(
        [
            ref[(group * per_group + r) * HEAD : (group * per_group + r + 1) * HEAD, :]
            for r in range(per_group)
        ],
        axis=1,
    )


def slot_columns(ref, first, count, row):
    return jnp.concatenate(
        [ref[first + s, row : row + HEAD, :] for s in range(count)], axis=1
    )


def attend_kernel(groups, per_group, chunk, q_ref, kv_ref, bias_ref, o_ref, lse_ref):
    rows = q_ref.shape[1]
    slots = kv_ref.shape[0]
    wide = per_group * rows
    for group in range(groups):
        q = group_columns(q_ref, group, per_group)

        def step(index, running):
            first = index * chunk
            k = slot_columns(kv_ref, first, chunk, group * HEAD)
            v = slot_columns(kv_ref, first, chunk, (groups + group) * HEAD)
            bias = bias_ref[pl.ds(first * rows, chunk * rows), :]
            s = mm(k, q, 0, 0) + jnp.concatenate([bias] * per_group, axis=1)
            top = jnp.max(s, axis=0, keepdims=True)
            if running is not None:
                top = jnp.maximum(top, running[0])
            p = jnp.exp(s - top)
            total = jnp.sum(p, axis=0, keepdims=True)
            out = mm(v, p.astype(BF), 1, 0)
            if running is not None:
                shrink = jnp.exp(running[0] - top)
                total = total + running[1] * shrink
                out = out + running[2] * shrink
            return (top, total, out)

        if slots == chunk:
            top, total, out = step(0, None)
        else:
            top, total, out = lax.fori_loop(
                0,
                slots // chunk,
                step,
                (
                    jnp.full((1, wide), -1e30, F32),
                    jnp.zeros((1, wide), F32),
                    jnp.zeros((HEAD, wide), F32),
                ),
            )
        out = out / total
        lse = top + jnp.log(total)
        for r in range(per_group):
            head = group * per_group + r
            o_ref[head * HEAD : (head + 1) * HEAD, :] = out[:, r * rows : (r + 1) * rows]
            lse_ref[head : head + 1, :] = lse[:, r * rows : (r + 1) * rows]


def attend_back_kernel(
    groups, per_group, chunk, q_ref, kv_ref, bias_ref, lse_ref, do_ref, o_ref, dq_ref, dkv_ref
):
    rows = q_ref.shape[1]
    slots = kv_ref.shape[0]
    wide = per_group * rows
    for group in range(groups):
        q = group_columns(q_ref, group, per_group)
        do = group_columns(do_ref, group, per_group)
        o = group_columns(o_ref, group, per_group)
        delta = jnp.sum(do.astype(F32) * o, axis=0, keepdims=True)
        lse = jnp.concatenate(
            [
                lse_ref[group * per_group + r : group * per_group + r + 1, :]
                for r in range(per_group)
            ],
            axis=1,
        )

        def step(index, dq):
            first = index * chunk
            k = slot_columns(kv_ref, first, chunk, group * HEAD)
            v = slot_columns(kv_ref, first, chunk, (groups + group) * HEAD)
            bias = bias_ref[pl.ds(first * rows, chunk * rows), :]
            s = mm(k, q, 0, 0) + jnp.concatenate([bias] * per_group, axis=1)
            p = jnp.exp(s - lse)
            dp = mm(v, do, 0, 0)
            ds = (p * (dp - delta)).astype(BF)
            dk = mm(q, ds, 1, 1).astype(BF)
            dv = mm(do, p.astype(BF), 1, 1).astype(BF)
            for s_index in range(chunk):
                columns = slice(s_index * rows, (s_index + 1) * rows)
                dkv_ref[first + s_index, group * HEAD : (group + 1) * HEAD, :] = dk[:, columns]
                dkv_ref[
                    first + s_index, (groups + group) * HEAD : (groups + group + 1) * HEAD, :
                ] = dv[:, columns]
            return dq + mm(k, ds, 1, 0)

        dq = jnp.zeros((HEAD, wide), F32)
        dq = step(0, dq) if slots == chunk else lax.fori_loop(0, slots // chunk, step, dq)
        dq = dq * HEAD ** (-0.5)
        for r in range(per_group):
            head = group * per_group + r
            dq_ref[head * HEAD : (head + 1) * HEAD, :] = dq[:, r * rows : (r + 1) * rows]


def attend(groups, per_group, q, kv, bias):
    rows, slots = q.shape[1], kv.shape[0]
    heads = groups * per_group
    cost = pl.CostEstimate(
        flops=4 * heads * HEAD * rows * rows * slots * 2,
        bytes_accessed=q.size * 6 + kv.size * 2 + bias.size * 4,
        transcendentals=heads * rows * rows * slots,
    )
    return pl.pallas_call(
        functools.partial(attend_kernel, groups, per_group, min(slots, 8)),
        out_shape=(
            jax.ShapeDtypeStruct(q.shape, F32),
            jax.ShapeDtypeStruct((heads, rows), F32),
        ),
        cost_estimate=cost,
        compiler_params=pltpu.CompilerParams(vmem_limit_bytes=VMEM_LIMIT),
    )(q, kv, bias)


def attend_back(groups, per_group, q, kv, bias, lse, do, o):
    rows, slots = q.shape[1], kv.shape[0]
    heads = groups * per_group
    cost = pl.CostEstimate(
        flops=10 * heads * HEAD * rows * rows * slots * 2,
        bytes_accessed=q.size * 12 + kv.size * 4 + bias.size * 4,
        transcendentals=heads * rows * rows * slots,
    )
    return pl.pallas_call(
        functools.partial(attend_back_kernel, groups, per_group, min(slots, 8)),
        out_shape=(
            jax.ShapeDtypeStruct(q.shape, F32),
            jax.ShapeDtypeStruct(kv.shape, BF),
        ),
        cost_estimate=cost,
        compiler_params=pltpu.CompilerParams(vmem_limit_bytes=VMEM_LIMIT),
    )(q, kv, bias, lse, do, o)


def rms(x, gain):
    r = lax.rsqrt(jnp.mean(x * x, axis=-1, keepdims=True) + EPS)
    return x * r * gain, r


def rms_back(dh, x, r, gain):
    xn = x * r
    d_gain = jnp.sum(dh * xn, axis=0)
    dxn = dh * gain
    return r * (dxn - xn * jnp.mean(dxn * xn, axis=-1, keepdims=True)), d_gain


def turn(z, cosines, sines, back=False):
    if back:
        sines = -sines
    half = HEAD // 2
    parts = z.reshape(z.shape[0] // HEAD, HEAD, z.shape[1])
    a, b = parts[:, :half], parts[:, half:]
    return jnp.concatenate([a * cosines - b * sines, b * cosines + a * sines], axis=1).reshape(
        z.shape
    )


def local(
    n_ctx,
    n_wa,
    tokens,
    w_query,
    w_key,
    w_value,
    w_out,
    w_gate,
    w_up,
    w_down,
    norm_attn,
    norm_ffn,
    cotangent,
):
    seqs, rows, width = tokens.shape
    q_width, k_width = w_query.shape[1], w_key.shape[1]
    per_group = q_width // k_width
    groups = k_width // HEAD
    shard = w_query.shape[0]
    ff_part = w_down.shape[0]
    c_bits = bits_of(n_ctx)
    each = range(seqs)
    here = lax.axis_index("ctx")

    gain_rows = jnp.pad(jnp.stack([norm_attn, norm_ffn]), ((0, 6), (0, 2 * k_width - shard)))
    kv_steps = gather_rows(
        jnp.concatenate([jnp.concatenate([w_key, w_value], axis=1), gain_rows], axis=0), n_wa, shard
    )
    got = next(kv_steps)
    q_steps = gather_rows(after(w_query, got), n_wa)
    got = next(q_steps)
    o_steps = gather_rows(after(w_out, got), n_wa)
    got = next(o_steps)
    w_gu = jnp.stack(
        [
            jnp.concatenate([w[:, j * ff_part : (j + 1) * ff_part] for w in (w_gate, w_up)], axis=1)
            for j in range(n_wa)
        ]
    )
    gu_steps = exchange_blocks(after(w_gu, got), n_wa)
    got = next(gu_steps)
    dy_all = gather_relative(after(cotangent, got)[None], n_wa)
    dy_all = [dy_all[:, i].reshape(-1, width) for i in each]
    w_kv, gains = complete(kv_steps)
    gains = gains[:, :2, :shard].transpose(1, 0, 2).reshape(2, width).astype(F32)

    half = HEAD // 2
    frequency = 10000.0 ** (-jnp.arange(half).astype(F32) / half)
    position = (here * rows + jnp.arange(rows, dtype=jnp.int32)).astype(F32)
    angles = frequency[:, None] * position[None, :]
    cosines, sines = lax.optimization_barrier((jnp.cos(angles), jnp.sin(angles)))
    high_first = list(reversed(range(c_bits)))
    low_swapped = high_first[:-2] + high_first[-2:][::-1]
    orders = [high_first if i % 2 == 0 else low_swapped for i in each]

    def bias_of(order):
        block = here ^ jnp.array(slot_offsets(order), jnp.int32)
        key_place = (block[:, None] * rows + jnp.arange(rows, dtype=jnp.int32)[None, :]).reshape(-1)
        query_place = here * rows + jnp.arange(rows, dtype=jnp.int32)
        return jnp.where(key_place[:, None] <= query_place[None, :], 0.0, -1e30).astype(F32)

    biases = [bias_of(order) for order in orders]

    x, h1, r1, kv = [], [], [], []
    for i in each:
        xi = tokens[i].astype(F32)
        hi, ri = rms(xi, gains[0])
        hi = hi.astype(BF)
        kvi = mm(w_kv, hi, 0, 1)
        ki = turn(kvi[:k_width], cosines, sines).astype(BF)
        vi = kvi[k_width:].astype(BF)
        x.append(xi)
        h1.append(hi)
        r1.append(ri)
        kv.append(Chain(doubled(jnp.concatenate([ki, vi], axis=0)[None], n_ctx, orders[i])))
    sent = [chain.pending for chain in kv]
    for chain in kv:
        chain.issue()
    w_q, _ = complete(q_steps, sent)
    q = [
        turn(mm(w_q, hi, 0, 1), cosines, sines).astype(BF) * BF(HEAD ** (-0.5)) for hi in h1
    ]
    sent = [chain.pending for chain in kv]
    for chain in kv:
        chain.issue()
    w_o, _ = complete(o_steps, sent)
    sent = [chain.pending for chain in kv]
    w_gu = complete(gu_steps, sent).reshape(width, 2 * ff_part)
    kv = [chain.finish() for chain in kv]

    o, lse, o_b, x1, r2, h2_all = [], [], [], [], [], []
    for i in each:
        oi, li = attend(groups, per_group, q[i], kv[i], biases[i])
        ob = oi.astype(BF)
        x1i = x[i] + mm(ob, w_o, 0, 0)
        h2, r2i = rms(x1i, gains[1])
        o.append(oi)
        lse.append(li)
        o_b.append(ob)
        x1.append(x1i)
        r2.append(r2i)
        h2_all.append(gather_relative(h2.astype(BF), n_wa))

    mixed, dh2, act_all, dgu_all = [], [], [], []
    for i in each:
        gu = mm(h2_all[i], w_gu, 1, 0)
        gate, up = gu[:, :ff_part], gu[:, ff_part:]
        sig = jax.nn.sigmoid(gate)
        silu = gate * sig
        act = (silu * up).astype(BF)
        dact = mm(dy_all[i], w_down, 1, 1)
        dgate = (dact * up * sig * (1.0 + gate * (1.0 - sig))).astype(BF)
        dup = (dact * silu).astype(BF)
        dgu = jnp.concatenate([dgate, dup], axis=1)
        dh2.append(scatter_relative(mm(dgu, w_gu, 1, 1), n_wa))
        mixed.append((x1[i] + scatter_relative(mm(act, w_down, 1, 0), n_wa)).astype(BF))
        act_all.append(act)
        dgu_all.append(dgu)
    act_all = jnp.concatenate(act_all, axis=0)
    dgu_all = jnp.concatenate(dgu_all, axis=0)
    h2_cat = jnp.concatenate(h2_all, axis=0)
    dy_cat = jnp.concatenate(dy_all, axis=0)

    low_first = list(range(c_bits))
    g_gu = mm(h2_cat, dgu_all, 0, 0).astype(BF).reshape(n_wa, shard, 2 * ff_part)
    g_down = mm(act_all, dy_cat, 0, 0).astype(BF)
    g_down_sum = lax.psum(g_down, "ctx")
    g_gu_sum = lax.psum(g_gu, "ctx")
    dh2[0] = after(dh2[0], g_gu)
    dh2[0] = after(dh2[0], g_down)

    dx1, dx1_b, dq_b, dkv, dg2, do = [], [], [], [], [], []
    for i in each:
        norm_part, dgi = rms_back(dh2[i], x1[i], r2[i], gains[1])
        dx1i = cotangent[i].astype(F32) + norm_part
        dx1b = dx1i.astype(BF)
        dx1.append(dx1i)
        dx1_b.append(dx1b)
        dg2.append(dgi)
        do.append(mm(w_o, dx1b, 1, 1).astype(BF))
    for i in each:
        doi = do[i]
        if i > 0:
            doi = dkv[-1].issue(doi)
        dqi, dkvi = attend_back(groups, per_group, q[i], kv[i], biases[i], lse[i], doi, o[i])
        dq_b.append(turn(dqi, cosines, sines, back=True).astype(BF))
        dkv.append(Chain(halved(dkvi, n_ctx, orders[i])))

    h1_cat = jnp.concatenate(h1, axis=0)
    dx1_cat = dkv[-1].issue(jnp.concatenate(dx1_b, axis=0))
    g_out = mm(jnp.concatenate(o_b, axis=1), dx1_cat, 1, 0)
    g_query = mm(h1_cat, jnp.concatenate(dq_b, axis=1), 0, 1)
    g_oq = jnp.concatenate([g_out, g_query], axis=1).astype(BF).reshape(n_wa, shard, -1)
    oq = Chain(all_reduce_rows(g_oq, n_wa, n_ctx, low_first))
    dkv[0].pending = oq.issue(dkv[0].pending)
    for chain in dkv:
        chain.issue()
    dkv[0].pending = oq.issue(dkv[0].pending)
    dkv = [chain.finish() for chain in dkv]
    dkv[0] = oq.issue(dkv[0])

    input_grad, dkv_b, dg1 = [], [], []
    for i in each:
        dk = turn(dkv[i][0, :k_width], cosines, sines, back=True)
        dkvb = jnp.concatenate([dk, dkv[i][0, k_width:]], axis=0).astype(BF)
        dh1 = mm(dq_b[i], w_q, 0, 1) + mm(dkvb, w_kv, 0, 1)
        norm_part, dgi = rms_back(dh1, x[i], r1[i], gains[0])
        input_grad.append((dx1[i] + norm_part).astype(BF))
        dkv_b.append(dkvb)
        dg1.append(dgi)
    g_kv = mm(h1_cat, jnp.concatenate(dkv_b, axis=1), 0, 1).reshape(n_wa, shard, -1)
    g_gain = jnp.stack([sum(dg1), sum(dg2)]).reshape(2, n_wa, shard).transpose(1, 0, 2)
    g_gain = jnp.pad(g_gain, ((0, 0), (0, 6), (0, g_kv.shape[2] - shard)))
    g_kv = jnp.concatenate([g_kv, g_gain], axis=1).astype(BF)
    kvw = Chain(all_reduce_rows(g_kv, n_wa, n_ctx, low_first))
    kvw.pending = oq.issue(kvw.pending)
    g_oq, g_kv = [chain.finish().astype(F32) for chain in (oq, kvw)]
    g_down = g_down_sum.astype(F32)
    gu_steps = exchange_blocks(g_gu_sum, n_wa)
    next(gu_steps)
    g_gu = complete(gu_steps)
    g_gate, g_up = [
        g_gu[:, :, s * ff_part : (s + 1) * ff_part]
        .transpose(1, 0, 2)
        .reshape(shard, n_wa * ff_part)
        .astype(F32)
        for s in range(2)
    ]

    return (
        jnp.stack(mixed),
        jnp.stack(input_grad),
        g_oq[:, width:],
        g_kv[:shard, :k_width],
        g_kv[:shard, k_width:],
        g_oq[:, :width],
        g_gate,
        g_up,
        g_down,
        g_kv[shard, :shard],
        g_kv[shard + 1, :shard],
    )


def solution(mesh):
    rows, weight, vector = P("wa", "ctx", None), P("wa", None), P("wa")
    specs = (weight,) * 7 + (vector,) * 2
    return jax.shard_map(
        functools.partial(local, mesh.shape["ctx"], mesh.shape["wa"]),
        mesh=mesh,
        in_specs=(rows,) + specs + (rows,),
        out_specs=(rows, rows) + specs,
        check_vma=False,
    )
```

```python
import functools

import jax
import jax.numpy as jnp
from jax import lax
from jax.experimental import pallas as pl
from jax.experimental.pallas import tpu as pltpu
from jax.sharding import PartitionSpec as P

HEAD = 64
EPS = 1e-05
BF = jnp.bfloat16
F32 = jnp.float32
VMEM_LIMIT = 60 * 1024 * 1024


def mm(a, b, ca, cb):
    return lax.dot_general(a, b, (((ca,), (cb,)), ((), ())), preferred_element_type=F32)


def bits_of(n):
    return max(n - 1, 0).bit_length()


def swap(a, axis, n, bit):
    return lax.ppermute(a, axis, [(i, i ^ (1 << bit)) for i in range(n)])


def my_bit(axis, bit):
    return (lax.axis_index(axis) >> bit) & 1


def ordered(mine, theirs, bit, dim):
    return jnp.where(
        bit == 0,
        jnp.concatenate([mine, theirs], axis=dim),
        jnp.concatenate([theirs, mine], axis=dim),
    )


def after(value, other):
    return lax.optimization_barrier((value, other))[0]


class Chain:
    def __init__(self, steps):
        self.steps = steps
        self.pending = next(steps)
        self.result = None

    def issue(self, value=None):
        if self.pending is None:
            return value
        if value is not None:
            value = after(value, self.pending)
        try:
            self.pending = self.steps.send(self.pending)
        except StopIteration as stop:
            self.pending, self.result = None, stop.value
        return value

    def finish(self):
        while self.pending is not None:
            self.issue()
        return self.result


def gather_rows(a, n, lead=None):
    lead = lead or a.shape[0]
    nb = bits_of(n)
    out = a.reshape((1,) * nb + a.shape)
    for bit in reversed(range(nb)):
        dim, mine = nb - 1 - bit, my_bit("wa", bit)
        got = swap(out, "wa", n, bit)
        wait = yield got
        got = got if wait is None else after(got, wait)
        if bit == 0:
            rest = ordered(out[..., lead:, :], got[..., lead:, :], mine, dim)
            out, got = out[..., :lead, :], got[..., :lead, :]
        out = ordered(out, got, mine, dim)
    return out.reshape(-1, a.shape[1]), rest.reshape(n, -1, a.shape[1])


def gather_relative(a, n):
    blocks = {0: a}
    for bit in reversed(range(bits_of(n))):
        for place in list(blocks):
            blocks[place | (1 << bit)] = swap(blocks[place], "wa", n, bit)
    return jnp.concatenate(list(blocks.values()), axis=0)


def scatter_relative(a, n):
    for bit in range(bits_of(n)):
        half = a.shape[0] // 2
        a = a[:half] + swap(a[half:].astype(BF), "wa", n, bit).astype(F32)
    return a


def scatter_rows(a, n):
    nb = bits_of(n)
    a = a.reshape((2,) * nb + a.shape[1:])
    for bit in range(nb):
        dim = nb - 1 - bit
        mine = my_bit("wa", bit)
        keep = lax.dynamic_slice_in_dim(a, mine, 1, dim)
        send = lax.dynamic_slice_in_dim(a, 1 - mine, 1, dim).astype(BF)
        send = yield send
        a = (keep.astype(F32) + swap(send, "wa", n, bit).astype(F32)).astype(BF)
    return a.reshape(a.shape[nb:])


def exchange_blocks(a, n):
    nb = bits_of(n)
    out = a.reshape((2,) * nb + a.shape[1:])
    for bit in reversed(range(nb)):
        dim, mine = nb - 1 - bit, my_bit("wa", bit)
        keep = lax.dynamic_slice_in_dim(out, mine, 1, dim)
        got = swap(lax.dynamic_slice_in_dim(out, 1 - mine, 1, dim), "wa", n, bit)
        wait = yield got
        got = got if wait is None else after(got, wait)
        out = ordered(keep, got, mine, dim)
    return out.reshape(a.shape)


def complete(steps, wait=None):
    try:
        steps.send(wait)
        while True:
            next(steps)
    except StopIteration as stop:
        return stop.value


def all_reduce_ctx(a, n, plan):
    trail = []
    for bit in plan:
        size = a.shape[0]
        half = -(-size // 16) * 8
        mine = my_bit("ctx", bit)
        if half >= size:
            send = a.astype(BF)
            yield send
            a = (a.astype(F32) + swap(send, "ctx", n, bit).astype(F32)).astype(BF)
            continue
        keep = lax.dynamic_slice_in_dim(a, mine * (size - half), half, 0)
        send = lax.dynamic_slice_in_dim(a, (1 - mine) * (size - half), half, 0).astype(BF)
        yield send
        a = (keep.astype(F32) + swap(send, "ctx", n, bit).astype(F32)).astype(BF)
        trail.append((bit, size))
    for bit, size in reversed(trail):
        yield a
        got = swap(a, "ctx", n, bit)
        mine = my_bit("ctx", bit)
        extra = 2 * a.shape[0] - size
        if extra == 0:
            a = ordered(a, got, mine, 0)
        else:
            low = jnp.where(mine == 0, a, got)
            high = jnp.where(mine == 0, got, a)
            a = jnp.concatenate([low, high[extra:]], axis=0)
    return a


def all_reduce_rows(a, n_wa, n_ctx, plan):
    own = yield from scatter_rows(a, n_wa)
    return (yield from all_reduce_ctx(own, n_ctx, plan))


def doubled(a, n, order):
    for bit in order:
        yield a
        a = jnp.concatenate([a, swap(a, "ctx", n, bit)], axis=0)
    return a


def halved(a, n, order):
    for bit in reversed(order):
        half = a.shape[0] // 2
        send = yield a[half:]
        got = swap(send, "ctx", n, bit)
        a = (a[:half].astype(F32) + got.astype(F32)).astype(BF if half > 1 else F32)
    return a


def slot_offsets(order):
    offsets = [0]
    for bit in order:
        offsets = offsets + [offset ^ (1 << bit) for offset in offsets]
    return offsets


def group_columns(ref, group, per_group):
    return jnp.concatenate(
        [
            ref[(group * per_group + r) * HEAD : (group * per_group + r + 1) * HEAD, :]
            for r in range(per_group)
        ],
        axis=1,
    )


def slot_columns(ref, first, count, row):
    return jnp.concatenate(
        [ref[first + s, row : row + HEAD, :] for s in range(count)], axis=1
    )


def attend_kernel(groups, per_group, chunk, q_ref, kv_ref, bias_ref, o_ref, lse_ref):
    rows = q_ref.shape[1]
    slots = kv_ref.shape[0]
    wide = per_group * rows
    for group in range(groups):
        q = group_columns(q_ref, group, per_group)

        def step(index, running):
            first = index * chunk
            k = slot_columns(kv_ref, first, chunk, group * HEAD)
            v = slot_columns(kv_ref, first, chunk, (groups + group) * HEAD)
            bias = bias_ref[pl.ds(first * rows, chunk * rows), :]
            s = mm(k, q, 0, 0) + jnp.concatenate([bias] * per_group, axis=1)
            top = jnp.max(s, axis=0, keepdims=True)
            if running is not None:
                top = jnp.maximum(top, running[0])
            p = jnp.exp(s - top)
            total = jnp.sum(p, axis=0, keepdims=True)
            out = mm(v, p.astype(BF), 1, 0)
            if running is not None:
                shrink = jnp.exp(running[0] - top)
                total = total + running[1] * shrink
                out = out + running[2] * shrink
            return (top, total, out)

        if slots == chunk:
            top, total, out = step(0, None)
        else:
            top, total, out = lax.fori_loop(
                0,
                slots // chunk,
                step,
                (
                    jnp.full((1, wide), -1e30, F32),
                    jnp.zeros((1, wide), F32),
                    jnp.zeros((HEAD, wide), F32),
                ),
            )
        out = out / total
        lse = top + jnp.log(total)
        for r in range(per_group):
            head = group * per_group + r
            o_ref[head * HEAD : (head + 1) * HEAD, :] = out[:, r * rows : (r + 1) * rows]
            lse_ref[head : head + 1, :] = lse[:, r * rows : (r + 1) * rows]


def attend_back_kernel(
    groups, per_group, chunk, q_ref, kv_ref, bias_ref, lse_ref, do_ref, o_ref, dq_ref, dkv_ref
):
    rows = q_ref.shape[1]
    slots = kv_ref.shape[0]
    wide = per_group * rows
    for group in range(groups):
        q = group_columns(q_ref, group, per_group)
        do = group_columns(do_ref, group, per_group)
        o = group_columns(o_ref, group, per_group)
        delta = jnp.sum(do.astype(F32) * o, axis=0, keepdims=True)
        lse = jnp.concatenate(
            [
                lse_ref[group * per_group + r : group * per_group + r + 1, :]
                for r in range(per_group)
            ],
            axis=1,
        )

        def step(index, dq):
            first = index * chunk
            k = slot_columns(kv_ref, first, chunk, group * HEAD)
            v = slot_columns(kv_ref, first, chunk, (groups + group) * HEAD)
            bias = bias_ref[pl.ds(first * rows, chunk * rows), :]
            s = mm(k, q, 0, 0) + jnp.concatenate([bias] * per_group, axis=1)
            p = jnp.exp(s - lse)
            dp = mm(v, do, 0, 0)
            ds = (p * (dp - delta)).astype(BF)
            dk = mm(q, ds, 1, 1).astype(BF)
            dv = mm(do, p.astype(BF), 1, 1).astype(BF)
            for s_index in range(chunk):
                columns = slice(s_index * rows, (s_index + 1) * rows)
                dkv_ref[first + s_index, group * HEAD : (group + 1) * HEAD, :] = dk[:, columns]
                dkv_ref[
                    first + s_index, (groups + group) * HEAD : (groups + group + 1) * HEAD, :
                ] = dv[:, columns]
            return dq + mm(k, ds, 1, 0)

        dq = jnp.zeros((HEAD, wide), F32)
        dq = step(0, dq) if slots == chunk else lax.fori_loop(0, slots // chunk, step, dq)
        dq = dq * HEAD ** (-0.5)
        for r in range(per_group):
            head = group * per_group + r
            dq_ref[head * HEAD : (head + 1) * HEAD, :] = dq[:, r * rows : (r + 1) * rows]


def attend(groups, per_group, q, kv, bias):
    rows, slots = q.shape[1], kv.shape[0]
    heads = groups * per_group
    cost = pl.CostEstimate(
        flops=4 * heads * HEAD * rows * rows * slots * 2,
        bytes_accessed=q.size * 6 + kv.size * 2 + bias.size * 4,
        transcendentals=heads * rows * rows * slots,
    )
    return pl.pallas_call(
        functools.partial(attend_kernel, groups, per_group, min(slots, 8)),
        out_shape=(
            jax.ShapeDtypeStruct(q.shape, F32),
            jax.ShapeDtypeStruct((heads, rows), F32),
        ),
        cost_estimate=cost,
        compiler_params=pltpu.CompilerParams(vmem_limit_bytes=VMEM_LIMIT),
    )(q, kv, bias)


def attend_back(groups, per_group, q, kv, bias, lse, do, o):
    rows, slots = q.shape[1], kv.shape[0]
    heads = groups * per_group
    cost = pl.CostEstimate(
        flops=10 * heads * HEAD * rows * rows * slots * 2,
        bytes_accessed=q.size * 12 + kv.size * 4 + bias.size * 4,
        transcendentals=heads * rows * rows * slots,
    )
    return pl.pallas_call(
        functools.partial(attend_back_kernel, groups, per_group, min(slots, 8)),
        out_shape=(
            jax.ShapeDtypeStruct(q.shape, F32),
            jax.ShapeDtypeStruct(kv.shape, BF),
        ),
        cost_estimate=cost,
        compiler_params=pltpu.CompilerParams(vmem_limit_bytes=VMEM_LIMIT),
    )(q, kv, bias, lse, do, o)


def rms(x, gain):
    r = lax.rsqrt(jnp.mean(x * x, axis=-1, keepdims=True) + EPS)
    return x * r * gain, r


def rms_back(dh, x, r, gain):
    xn = x * r
    d_gain = jnp.sum(dh * xn, axis=0)
    dxn = dh * gain
    return r * (dxn - xn * jnp.mean(dxn * xn, axis=-1, keepdims=True)), d_gain


def turn(z, cosines, sines, back=False):
    if back:
        sines = -sines
    half = HEAD // 2
    parts = z.reshape(z.shape[0] // HEAD, HEAD, z.shape[1])
    a, b = parts[:, :half], parts[:, half:]
    return jnp.concatenate([a * cosines - b * sines, b * cosines + a * sines], axis=1).reshape(
        z.shape
    )


def local(
    n_ctx,
    n_wa,
    tokens,
    w_query,
    w_key,
    w_value,
    w_out,
    w_gate,
    w_up,
    w_down,
    norm_attn,
    norm_ffn,
    cotangent,
):
    seqs, rows, width = tokens.shape
    q_width, k_width = w_query.shape[1], w_key.shape[1]
    per_group = q_width // k_width
    groups = k_width // HEAD
    shard = w_query.shape[0]
    ff_part = w_down.shape[0]
    c_bits = bits_of(n_ctx)
    each = range(seqs)
    here = lax.axis_index("ctx")

    gain_rows = jnp.pad(jnp.stack([norm_attn, norm_ffn]), ((0, 6), (0, 2 * k_width - shard)))
    kv_steps = gather_rows(
        jnp.concatenate([jnp.concatenate([w_key, w_value], axis=1), gain_rows], axis=0), n_wa, shard
    )
    got = next(kv_steps)
    q_steps = gather_rows(after(w_query, got), n_wa)
    got = next(q_steps)
    o_steps = gather_rows(after(w_out, got), n_wa)
    got = next(o_steps)
    w_gu = jnp.stack(
        [
            jnp.concatenate([w[:, j * ff_part : (j + 1) * ff_part] for w in (w_gate, w_up)], axis=1)
            for j in range(n_wa)
        ]
    )
    gu_steps = exchange_blocks(after(w_gu, got), n_wa)
    got = next(gu_steps)
    dy_all = gather_relative(after(cotangent, got)[None], n_wa)
    dy_all = [dy_all[:, i].reshape(-1, width) for i in each]
    w_kv, gains = complete(kv_steps)
    gains = gains[:, :2, :shard].transpose(1, 0, 2).reshape(2, width).astype(F32)

    half = HEAD // 2
    frequency = 10000.0 ** (-jnp.arange(half).astype(F32) / half)
    position = (here * rows + jnp.arange(rows, dtype=jnp.int32)).astype(F32)
    angles = frequency[:, None] * position[None, :]
    cosines, sines = lax.optimization_barrier((jnp.cos(angles), jnp.sin(angles)))
    high_first = list(reversed(range(c_bits)))
    low_swapped = high_first[:-2] + high_first[-2:][::-1]
    orders = [high_first if i % 2 == 0 else low_swapped for i in each]

    def bias_of(order):
        block = here ^ jnp.array(slot_offsets(order), jnp.int32)
        key_place = (block[:, None] * rows + jnp.arange(rows, dtype=jnp.int32)[None, :]).reshape(-1)
        query_place = here * rows + jnp.arange(rows, dtype=jnp.int32)
        return jnp.where(key_place[:, None] <= query_place[None, :], 0.0, -1e30).astype(F32)

    biases = [bias_of(order) for order in orders]

    x, h1, r1, kv = [], [], [], []
    for i in each:
        xi = tokens[i].astype(F32)
        hi, ri = rms(xi, gains[0])
        hi = hi.astype(BF)
        kvi = mm(w_kv, hi, 0, 1)
        ki = turn(kvi[:k_width], cosines, sines).astype(BF)
        vi = kvi[k_width:].astype(BF)
        x.append(xi)
        h1.append(hi)
        r1.append(ri)
        kv.append(Chain(doubled(jnp.concatenate([ki, vi], axis=0)[None], n_ctx, orders[i])))
    sent = [chain.pending for chain in kv]
    for chain in kv:
        chain.issue()
    w_q, _ = complete(q_steps, sent)
    q = [
        turn(mm(w_q, hi, 0, 1), cosines, sines).astype(BF) * BF(HEAD ** (-0.5)) for hi in h1
    ]
    sent = [chain.pending for chain in kv]
    for chain in kv:
        chain.issue()
    w_o, _ = complete(o_steps, sent)
    sent = [chain.pending for chain in kv]
    w_gu = complete(gu_steps, sent).reshape(width, 2 * ff_part)
    kv = [chain.finish() for chain in kv]

    o, lse, o_b, x1, r2, h2_all = [], [], [], [], [], []
    for i in each:
        oi, li = attend(groups, per_group, q[i], kv[i], biases[i])
        ob = oi.astype(BF)
        x1i = x[i] + mm(ob, w_o, 0, 0)
        h2, r2i = rms(x1i, gains[1])
        o.append(oi)
        lse.append(li)
        o_b.append(ob)
        x1.append(x1i)
        r2.append(r2i)
        h2_all.append(gather_relative(h2.astype(BF), n_wa))

    mixed, dh2, act_all, dgu_all = [], [], [], []
    for i in each:
        gu = mm(h2_all[i], w_gu, 1, 0)
        gate, up = gu[:, :ff_part], gu[:, ff_part:]
        sig = jax.nn.sigmoid(gate)
        silu = gate * sig
        act = (silu * up).astype(BF)
        dact = mm(dy_all[i], w_down, 1, 1)
        dgate = (dact * up * sig * (1.0 + gate * (1.0 - sig))).astype(BF)
        dup = (dact * silu).astype(BF)
        dgu = jnp.concatenate([dgate, dup], axis=1)
        dh2.append(scatter_relative(mm(dgu, w_gu, 1, 1), n_wa))
        mixed.append((x1[i] + scatter_relative(mm(act, w_down, 1, 0), n_wa)).astype(BF))
        act_all.append(act)
        dgu_all.append(dgu)
    act_all = jnp.concatenate(act_all, axis=0)
    dgu_all = jnp.concatenate(dgu_all, axis=0)
    h2_cat = jnp.concatenate(h2_all, axis=0)
    dy_cat = jnp.concatenate(dy_all, axis=0)

    low_first = list(range(c_bits))
    g_gu = mm(h2_cat, dgu_all, 0, 0).astype(BF).reshape(n_wa, shard, 2 * ff_part)
    g_down = mm(act_all, dy_cat, 0, 0).astype(BF)
    g_down_sum = lax.psum(g_down, "ctx")
    g_gu_sum = lax.psum(g_gu, "ctx")
    dh2[0] = after(dh2[0], g_gu)
    dh2[0] = after(dh2[0], g_down)

    dx1, dx1_b, dq_b, dkv, dg2, do = [], [], [], [], [], []
    for i in each:
        norm_part, dgi = rms_back(dh2[i], x1[i], r2[i], gains[1])
        dx1i = cotangent[i].astype(F32) + norm_part
        dx1b = dx1i.astype(BF)
        dx1.append(dx1i)
        dx1_b.append(dx1b)
        dg2.append(dgi)
        do.append(mm(w_o, dx1b, 1, 1).astype(BF))
    for i in each:
        doi = do[i]
        if i > 0:
            doi = dkv[-1].issue(doi)
        dqi, dkvi = attend_back(groups, per_group, q[i], kv[i], biases[i], lse[i], doi, o[i])
        dq_b.append(turn(dqi, cosines, sines, back=True).astype(BF))
        dkv.append(Chain(halved(dkvi, n_ctx, orders[i])))

    h1_cat = jnp.concatenate(h1, axis=0)
    dx1_cat = dkv[-1].issue(jnp.concatenate(dx1_b, axis=0))
    g_out = mm(jnp.concatenate(o_b, axis=1), dx1_cat, 1, 0)
    g_query = mm(h1_cat, jnp.concatenate(dq_b, axis=1), 0, 1)
    g_oq = jnp.concatenate([g_out, g_query], axis=1).astype(BF).reshape(n_wa, shard, -1)
    oq = Chain(all_reduce_rows(g_oq, n_wa, n_ctx, low_first[1:] + low_first[:1]))
    dkv[0].pending = oq.issue(dkv[0].pending)
    for chain in dkv:
        chain.issue()
    dkv[0].pending = oq.issue(dkv[0].pending)
    dkv = [chain.finish() for chain in dkv]
    dkv[0] = oq.issue(dkv[0])

    input_grad, dkv_b, dg1 = [], [], []
    for i in each:
        dk = turn(dkv[i][0, :k_width], cosines, sines, back=True)
        dkvb = jnp.concatenate([dk, dkv[i][0, k_width:]], axis=0).astype(BF)
        dh1 = mm(dq_b[i], w_q, 0, 1) + mm(dkvb, w_kv, 0, 1)
        norm_part, dgi = rms_back(dh1, x[i], r1[i], gains[0])
        input_grad.append((dx1[i] + norm_part).astype(BF))
        dkv_b.append(dkvb)
        dg1.append(dgi)
    g_kv = mm(h1_cat, jnp.concatenate(dkv_b, axis=1), 0, 1).reshape(n_wa, shard, -1)
    g_gain = jnp.stack([sum(dg1), sum(dg2)]).reshape(2, n_wa, shard).transpose(1, 0, 2)
    g_gain = jnp.pad(g_gain, ((0, 0), (0, 6), (0, g_kv.shape[2] - shard)))
    g_kv = jnp.concatenate([g_kv, g_gain], axis=1).astype(BF)
    kvw = Chain(all_reduce_rows(g_kv, n_wa, n_ctx, low_first))
    kvw.pending = oq.issue(kvw.pending)
    g_oq, g_kv = [chain.finish().astype(F32) for chain in (oq, kvw)]
    g_down = g_down_sum.astype(F32)
    gu_steps = exchange_blocks(g_gu_sum, n_wa)
    next(gu_steps)
    g_gu = complete(gu_steps)
    g_gate, g_up = [
        g_gu[:, :, s * ff_part : (s + 1) * ff_part]
        .transpose(1, 0, 2)
        .reshape(shard, n_wa * ff_part)
        .astype(F32)
        for s in range(2)
    ]

    return (
        jnp.stack(mixed),
        jnp.stack(input_grad),
        g_oq[:, width:],
        g_kv[:shard, :k_width],
        g_kv[:shard, k_width:],
        g_oq[:, :width],
        g_gate,
        g_up,
        g_down,
        g_kv[shard, :shard],
        g_kv[shard + 1, :shard],
    )


def solution(mesh):
    rows, weight, vector = P("wa", "ctx", None), P("wa", None), P("wa")
    specs = (weight,) * 7 + (vector,) * 2
    return jax.shard_map(
        functools.partial(local, mesh.shape["ctx"], mesh.shape["wa"]),
        mesh=mesh,
        in_specs=(rows,) + specs + (rows,),
        out_specs=(rows, rows) + specs,
        check_vma=False,
    )
```
